32 devices in a mesh: groups: 1, db: 16 (over z, y, core), seq: 2 (over x), mp: 1.
Axes of the slice: x: 2, y: 2, z: 4, core: 2. Of those that a mesh axis runs over, the one named last changes fastest.
Arguments:
- queries: bfloat16 [16, 896, 2048], P(('groups', 'db'), 'seq', 'mp'), may hold values from -110 to 110
- database: bfloat16 [64, 128, 896], P(('groups', 'db')), may hold values from -6 to 6
- nb_owner: int32 [16, 28], P(('groups', 'db'), 'seq'), may hold values from 0 to 15, as said below
- nb_row: int32 [16, 28], P(('groups', 'db'), 'seq'), may hold values from 0 to 3
- kv_weight: bfloat16 [896, 2, 2048], P('seq', None, 'mp'), may hold values from -0.1875 to 0.1875
Outputs:
- attended: bfloat16 [16, 896, 2048], P(('groups', 'db'), 'seq', 'mp')
The draws below stay inside these ranges and needn't reach their ends.
Inputs may be any that keep to these rules, and one draw needn't show every extreme that they name: `nb_owner`: within each device's aligned block of 14 consecutive slots of a sequence, no shard is named more than 2 times; one shard, the same for every block, is named exactly 2 times in every block.
All inputs are finite; a program needn't handle non-finite values.
Results may differ from the reference program's by a relative error of at most 0.015.
The reference program's roundings to bfloat16 on the way count: a program that leaves them out, or rounds other values in their place, can miss the bound.
Values may be sent and summed in bfloat16 or wider, within the bound.
A program may use at most 128 MiB of HBM per device.

```python
import jax
import jax.numpy as jnp
from jax import lax

HEADS = 16
HD = 128
ENC = 896
STRETCH = 64
NT = 128
KNN = 2
CH_DEV = 7
PASS_OWN = 4
SEQS = 16
STRETCHES = 14
LEN = 896
SLOTS = 28
PASSAGES = 64
CAP = 2
N_DB = 16
N_SEQ = 2


def draw_queries(key, part):
    key = jax.random.fold_in(key, 5)
    first = jax.random.fold_in(key, 0)
    base = jax.random.normal(first, (SEQS, LEN, HEADS * HD), jnp.float32)
    return jnp.clip(base, -5.0, 5.0).astype(jnp.bfloat16)


def draw_nb_owner(key, part):
    key = jax.random.fold_in(key, 7)
    hot_key, block_key = jax.random.split(key)
    per_block = KNN * CH_DEV
    hottest = jax.random.randint(hot_key, (), 0, N_DB).astype(jnp.int32)
    others = jnp.repeat((jnp.arange(N_DB - 1, dtype=jnp.int32) + hottest + 1) % N_DB, CAP)

    def one_block(block_seed):
        pick_key, order_key = jax.random.split(block_seed)
        chosen = jax.random.permutation(pick_key, others)[:per_block - CAP]
        filled = jnp.concatenate([jnp.full((CAP,), hottest, jnp.int32), chosen])
        return jax.random.permutation(order_key, filled)
    seeds = jax.random.split(block_key, SEQS * N_SEQ)
    return jax.vmap(one_block)(seeds).reshape(SEQS, SLOTS).astype(jnp.int32)


def set_ends(drawn, key, smallest, top_value):
    longest = drawn.shape.index(max(drawn.shape))
    spots = []
    for shift in (0, 1):
        where = [jax.random.randint(jax.random.fold_in(key, axis), (), 0, length) for axis, length in enumerate(drawn.shape)]
        where[longest] = (where[longest] + shift) % drawn.shape[longest]
        spots.append(tuple(where))
    return drawn.at[spots[0]].set(smallest).at[spots[1]].set(top_value)


def levels(stream_key, dims, pieces, smallest, largest):
    gain, own = 1.0, jax.random.fold_in(stream_key, 6)
    for dim, shards_of in pieces:
        draws = jnp.exp(jax.random.uniform(jax.random.fold_in(own, dim), (shards_of,), jnp.float32, smallest / len(pieces), largest / len(pieces)))
        gain = gain * jnp.repeat(draws, dims[dim] // shards_of).reshape([-1 if axis == dim else 1 for axis in range(len(dims))])
    return gain


def scatter_about(key, shape, scale, most, cuts=(), kind=jnp.bfloat16):
    factor_of = levels(key, shape, cuts, -0.22, 0.18) if cuts else 1.0
    array = jax.random.normal(key, shape, jnp.float32) * scale * factor_of
    return jnp.minimum(jnp.maximum(array, -most), most).astype(kind)


def setup_inputs(seed: int = 0, part: int = 0) -> dict:
    streams_of = jax.random.split(jax.random.key(seed), 6)
    part_splits = jax.random.split(jax.random.fold_in(streams_of[5], part), 6)
    queries = draw_queries(jax.random.fold_in(jax.random.fold_in(streams_of[5], part), 71), part)
    database = scatter_about(part_splits[1], (PASSAGES, NT, ENC), 1.0, 6.0, ((0, 16),))
    nb_owner = draw_nb_owner(jax.random.fold_in(jax.random.fold_in(streams_of[5], part), 71), part)
    nb_row = set_ends(jax.random.randint(part_splits[3], (SEQS, SLOTS), 0, PASS_OWN), jax.random.fold_in(part_splits[3], 1), 0, PASS_OWN - 1).astype(jnp.int32)
    kv_weight = scatter_about(streams_of[4], (ENC, 2, HEADS * HD), ENC ** -0.5, 0.1875, ((0, 2),))
    return dict(queries=queries, database=database, nb_owner=nb_owner, nb_row=nb_row, kv_weight=kv_weight)


def reference(queries, database, nb_owner, nb_row, kv_weight):
    weight_flat = kv_weight.reshape(ENC, 2 * HEADS * HD)
    passage_ids = (nb_owner * PASS_OWN + nb_row).astype(jnp.int32)

    def one_sequence(pair):
        query_rows, idents = pair
        fetched = jnp.take(database, idents, axis=0).reshape(SLOTS * NT, ENC)
        encoded = jnp.dot(fetched, weight_flat, preferred_element_type=jnp.float32).astype(jnp.bfloat16)
        encoded = encoded.reshape(STRETCHES, KNN * NT, 2, HEADS, HD)
        source = jnp.concatenate([jnp.zeros((1, KNN * NT, 2, HEADS, HD), jnp.bfloat16), encoded[:-1]], axis=0)
        query = query_rows.reshape(STRETCHES, STRETCH, HEADS, HD).astype(jnp.float32)
        keys = source[:, :, 0].astype(jnp.float32)
        values = source[:, :, 1].astype(jnp.float32)
        scores = jnp.einsum("cqhd,ckhd->chqk", query, keys) * (HD ** -0.5)
        top = jnp.max(scores, axis=-1, keepdims=True)
        weights = jnp.exp(scores - top)
        probs = (weights / jnp.sum(weights, axis=-1, keepdims=True)).astype(jnp.bfloat16)
        mixed = jnp.einsum("chqk,ckhd->cqhd", probs.astype(jnp.float32), values)
        return mixed.astype(jnp.bfloat16).reshape(LEN, HEADS * HD)

    return lax.map(one_sequence, (queries, passage_ids))
```

```python
import functools

import jax
import jax.numpy as jnp
from jax import lax
from jax.experimental import pallas as pl
from jax.experimental.pallas import tpu as pltpu
from jax.sharding import PartitionSpec as P

HD = 128
KNN = 2
MESH = pl.DeviceIdType.MESH


def attend(nz, ny, nc, nx, parts, *refs):
    q_hbm, db_hbm, ids_ref, w_hbm, out_ref = refs[:5]
    gathered = refs[5:5 + parts]
    (w_all, kv, q_all, rows, ids_in, ids_own_s, ids_in_s, z_send, z_recv, y_send, y_recv,
     c_send, c_recv, x_send, x_recv, wc_send, wc_recv, i_send, i_recv, local) = refs[5 + parts:]
    d = lax.axis_index("db")
    x = lax.axis_index("seq")
    core = lax.rem(d, nc)
    y = lax.rem(d // nc, ny)
    z = d // (nc * ny)
    held, tokens, enc = db_hbm.shape
    step = tokens // parts
    w_rows = w_hbm.shape[0]
    share = w_rows // nc
    slots = kv.shape[0]
    span = KNN * tokens
    cols = w_all.shape[1]
    width = cols // 2
    stretches = slots // KNN
    length = q_all.shape[0] // stretches

    def index(zz, yy, cc):
        return (zz * ny + yy) * nc + cc

    others_z = [lax.rem(z + r, nz) for r in range(1, nz)]
    other_y = lax.rem(y + 1, ny)
    sibling = index(z, y, lax.rem(core + 1, nc))
    others_x = [lax.rem(x + r, nx) for r in range(1, nx)]
    across_y = index(z, other_y, core)

    barrier = pltpu.get_barrier_semaphore()
    peers = [{"db": index(zz, y, core)} for zz in others_z]
    peers += [{"seq": xx} for xx in others_x]
    if ny > 1:
        peers.append({"db": across_y})
    if nc > 1:
        peers.append({"db": sibling})
    for peer in peers:
        pl.semaphore_signal(barrier, inc=1, device_id=peer, device_id_type=MESH)
    pl.semaphore_wait(barrier, len(peers))

    def cell(k, zz, yy, cc):
        return gathered[k].at[pl.ds(held * index(zz, yy, cc), held)]

    def mine(k):
        return db_hbm.at[:, pl.ds(k * step, step), :]

    def along_z(k, to, source):
        return pltpu.make_async_remote_copy(
            src_ref=mine(k), dst_ref=cell(k, source, y, core), send_sem=z_send.at[k, to],
            recv_sem=z_recv.at[k, source], device_id={"db": index(to, y, core)}, device_id_type=MESH)

    def along_y(k, zz, yy, own):
        return pltpu.make_async_remote_copy(
            src_ref=mine(k) if own else cell(k, zz, yy, core), dst_ref=cell(k, zz, yy, core),
            send_sem=y_send.at[k, zz], recv_sem=y_recv.at[k, zz],
            device_id={"db": across_y}, device_id_type=MESH)

    def to_core(k, zz, yy, cc, own):
        return pltpu.make_async_remote_copy(
            src_ref=mine(k) if own else cell(k, zz, yy, cc), dst_ref=cell(k, zz, yy, cc),
            send_sem=c_send.at[k, zz, yy], recv_sem=c_recv.at[k, zz, yy],
            device_id={"db": sibling}, device_id_type=MESH)

    def weight_rows(xx, cc):
        return w_all.at[pl.ds(pl.multiple_of(xx * w_rows + cc * share, 16), share)]

    def along_x(to, source):
        return pltpu.make_async_remote_copy(
            src_ref=w_hbm.at[pl.ds(pl.multiple_of(core * share, 16), share)], dst_ref=weight_rows(source, core),
            send_sem=x_send.at[to], recv_sem=x_recv.at[source],
            device_id={"seq": to}, device_id_type=MESH)

    def weight_to_core(xx, cc):
        return pltpu.make_async_remote_copy(
            src_ref=weight_rows(xx, cc), dst_ref=weight_rows(xx, cc),
            send_sem=wc_send.at[xx], recv_sem=wc_recv.at[xx],
            device_id={"db": sibling}, device_id_type=MESH)

    def send_own(k):
        for zz in others_z:
            along_z(k, zz, z).start()
        if ny > 1:
            along_y(k, z, y, True).start()
        if nc > 1:
            to_core(k, z, y, core, True).start()

    def pass_z(k):
        for zz in others_z:
            along_z(k, z, zz).wait_recv()
            if ny > 1:
                along_y(k, zz, y, False).start()
            if nc > 1:
                to_core(k, zz, y, core, False).start()

    def pass_y(k):
        if ny > 1:
            for zz in [z] + others_z:
                along_y(k, zz, other_y, False).wait_recv()
                if nc > 1:
                    to_core(k, zz, other_y, core, False).start()
        if nc > 1:
            cc = lax.rem(core + 1, nc)
            for yy in range(ny):
                for zz in range(nz):
                    to_core(k, zz, yy, cc, False).wait_recv()

    ids = pltpu.make_async_remote_copy(
        src_ref=ids_ref, dst_ref=ids_in, send_sem=i_send, recv_sem=i_recv,
        device_id={"seq": lax.rem(x + 1, nx)}, device_id_type=MESH)
    ids.start()
    for k in range(min(2, parts)):
        send_own(k)
        if k == 0:
            for xx in others_x:
                along_x(xx, x).start()
    stay = [pltpu.make_async_copy(mine(k), cell(k, z, y, core), local.at[k]) for k in range(parts)]
    stay.append(pltpu.make_async_copy(
        w_hbm, w_all.at[pl.ds(pl.multiple_of(x * w_rows, 16), w_rows)], local.at[parts]))
    stay.append(pltpu.make_async_copy(q_hbm.at[0], q_all, local.at[parts + 1]))
    stay.append(pltpu.make_async_copy(ids_ref, ids_own_s, local.at[parts + 2]))
    for copy in stay:
        copy.start()
    ids.wait()
    inward = pltpu.make_async_copy(ids_in, ids_in_s, local.at[parts + 3])
    inward.start()
    inward.wait()
    for copy in stay:
        copy.wait()

    def project(k):
        for j in range(slots):
            if j < KNN:
                block = gathered[k][ids_in_s[0, slots - KNN + j]]
                block = jnp.where(x > 0, block, jnp.zeros_like(block))
            else:
                block = gathered[k][ids_own_s[0, j - KNN]]
            rows[j * step:(j + 1) * step, :] = block
        tile = 512

        @pl.loop(0, cols // tile)
        def _(t):
            at = pl.ds(pl.multiple_of(t * tile, tile), tile)
            got = jnp.dot(rows[...], w_all[:, at], preferred_element_type=jnp.float32)
            kv[:, k * step:(k + 1) * step, at] = got.astype(jnp.bfloat16).reshape(slots, step, tile)

    for k in range(parts):
        if k + 2 < parts:
            send_own(k + 2)
        pass_z(k)
        if k == 1 or parts == 1:
            for xx in others_x:
                along_x(x, xx).wait_recv()
                if nc > 1:
                    weight_to_core(xx, core).start()
            if nc > 1:
                for xx in others_x:
                    weight_to_core(xx, lax.rem(core + 1, nc)).wait_recv()
        if k > 0:
            pass_y(k - 1)
            project(k - 1)
    pass_y(parts - 1)
    project(parts - 1)

    @pl.loop(0, stretches)
    def _(c):
        tok = pl.ds(pl.multiple_of(c * length, length), length)
        for h in range(width // HD):
            query = q_all[tok, h * HD:(h + 1) * HD]
            keys = kv[pl.ds(c * KNN, KNN), :, h * HD:(h + 1) * HD].reshape(span, HD)
            values = kv[pl.ds(c * KNN, KNN), :, width + h * HD:width + (h + 1) * HD].reshape(span, HD)
            scores = lax.dot_general(query, keys, (((1,), (1,)), ((), ())), preferred_element_type=jnp.float32)
            scores = scores * HD ** (-0.5)
            top = jnp.max(scores, axis=-1, keepdims=True)
            weights = jnp.exp(scores - top)
            probs = (weights / jnp.sum(weights, axis=-1, keepdims=True)).astype(jnp.bfloat16)
            mixed = jnp.dot(probs, values, preferred_element_type=jnp.float32)
            out_ref[0, tok, h * HD:(h + 1) * HD] = mixed.astype(jnp.bfloat16)

    for k in range(parts):
        for zz in others_z:
            along_z(k, zz, z).wait_send()
        if ny > 1:
            along_y(k, z, y, True).wait_send()
            for zz in others_z:
                along_y(k, zz, y, False).wait_send()
        if nc > 1:
            to_core(k, z, y, core, True).wait_send()
            for zz in others_z:
                to_core(k, zz, y, core, False).wait_send()
            for zz in [z] + others_z:
                if ny > 1:
                    to_core(k, zz, other_y, core, False).wait_send()
    for xx in others_x:
        along_x(xx, x).wait_send()
        if nc > 1:
            weight_to_core(xx, core).wait_send()


def solution(mesh):
    n_db, nx = mesh.shape["db"], mesh.shape["seq"]
    nc = 2 if mesh.shape["mp"] == 1 and n_db % 2 == 0 else 1
    ny = 2 if mesh.shape["groups"] == 1 and (n_db // nc) % 2 == 0 else 1
    nz = n_db // (nc * ny)
    parts = 4

    def per_device(queries, database, nb_owner, nb_row, kv_weight):
        held, tokens, enc = database.shape
        slots = nb_owner.shape[1]
        w_rows, _, head_cols = kv_weight.shape
        weight = kv_weight.reshape(w_rows, 2 * head_cols)
        ids = jnp.pad(nb_owner * held + nb_row, ((0, 7), (0, 128 - slots)))
        step = tokens // parts
        anywhere = pl.BlockSpec(memory_space=pl.ANY)
        vmem = pl.BlockSpec(memory_space=pltpu.VMEM)
        sem = pltpu.SemaphoreType.DMA
        flops = 2 * slots * tokens * enc * 2 * head_cols
        return pl.pallas_call(
            functools.partial(attend, nz, ny, nc, nx, parts),
            out_shape=jax.ShapeDtypeStruct(queries.shape, jnp.bfloat16),
            in_specs=[anywhere, anywhere, vmem, anywhere],
            out_specs=vmem,
            scratch_shapes=[pltpu.VMEM((n_db * held, step, enc), jnp.bfloat16) for _ in range(parts)] + [
                pltpu.VMEM((nx * w_rows, 2 * head_cols), jnp.bfloat16),
                pltpu.VMEM((slots, tokens, 2 * head_cols), jnp.bfloat16),
                pltpu.VMEM(queries.shape[1:], jnp.bfloat16),
                pltpu.VMEM((slots * step, enc), jnp.bfloat16),
                pltpu.VMEM((8, 128), jnp.int32),
                pltpu.SMEM((8, 128), jnp.int32),
                pltpu.SMEM((8, 128), jnp.int32),
                sem((parts, nz)), sem((parts, nz)),
                sem((parts, nz)), sem((parts, nz)),
                sem((parts, nz, ny)), sem((parts, nz, ny)),
                sem((nx,)), sem((nx,)),
                sem((nx,)), sem((nx,)),
                sem, sem,
                sem((parts + 4,)),
            ],
            compiler_params=pltpu.CompilerParams(
                collective_id=0, has_side_effects=True, vmem_limit_bytes=60 * 2 ** 20),
            cost_estimate=pl.CostEstimate(flops=flops, bytes_accessed=20 * 2 ** 20, transcendentals=0),
        )(queries, database, ids, weight)

    return jax.shard_map(
        per_device,
        mesh=mesh,
        in_specs=(
            P(("groups", "db"), "seq", "mp"),
            P(("groups", "db"), None, None),
            P(("groups", "db"), "seq"),
            P(("groups", "db"), "seq"),
            P("seq", None, "mp"),
        ),
        out_specs=P(("groups", "db"), "seq", "mp"),
        check_vma=False,
    )
```

```python
import functools

import jax
import jax.numpy as jnp
from jax import lax
from jax.experimental import pallas as pl
from jax.experimental.pallas import tpu as pltpu
from jax.sharding import PartitionSpec as P

HD = 128
KNN = 2
MESH = pl.DeviceIdType.MESH


def attend(nz, ny, nc, nx, parts, *refs):
    q_hbm, db_hbm, ids_ref, w_hbm, out_ref = refs[:5]
    gathered = refs[5:5 + parts]
    (w_all, kv, q_all, rows, ids_in, ids_own_s, ids_in_s, up_send, down_send, z_recv, y_send, y_recv,
     c_send, c_recv, a_send, a_recv, x_send, x_recv, wc_send, wc_recv, i_send, i_recv, local) = refs[5 + parts:]
    d = lax.axis_index("db")
    x = lax.axis_index("seq")
    core = lax.rem(d, nc)
    y = lax.rem(d // nc, ny)
    z = d // (nc * ny)
    held, tokens, enc = db_hbm.shape
    step = tokens // parts
    w_rows = w_hbm.shape[0]
    share = w_rows // nc
    slots = kv.shape[0]
    span = KNN * tokens
    cols = w_all.shape[1]
    width = cols // 2
    stretches = slots // KNN
    length = q_all.shape[0] // stretches
    other_y = lax.rem(y + 1, ny)
    other_core = lax.rem(core + 1, nc)
    skips = {0: (1, 3), 1: (2, 4)} if ny > 1 and nx == 2 and parts > 4 else {}
    skipper = {k: xx for xx, ks in skips.items() for k in ks}

    def index(zz, yy, cc):
        return (zz * ny + yy) * nc + cc

    others_x = [lax.rem(x + r, nx) for r in range(1, nx)]
    up, down = index(z + 1, y, core), index(z - 1, y, core)
    sibling = {"db": index(z, y, other_core)}
    across_y = {"db": index(z, other_y, core)}

    barrier = pltpu.get_barrier_semaphore()
    peers = [{"seq": xx} for xx in others_x]
    if ny > 1:
        peers.append(across_y)
    if nc > 1:
        peers.append(sibling)
    for peer in peers:
        pl.semaphore_signal(barrier, inc=1, device_id=peer, device_id_type=MESH)

    @pl.when(z < nz - 1)
    def _():
        pl.semaphore_signal(barrier, inc=1, device_id={"db": up}, device_id_type=MESH)

    @pl.when(z > 0)
    def _():
        pl.semaphore_signal(barrier, inc=1, device_id={"db": down}, device_id_type=MESH)

    ends = jnp.where((z == 0) | (z == nz - 1), 1, 0)
    pl.semaphore_wait(barrier, len(peers) + 2 - ends)

    def cell(k, zz, yy, cc):
        return gathered[k].at[pl.ds(held * ((cc * ny + yy) * nz + zz), held)]

    def column(k, yy, cc):
        return gathered[k].at[pl.ds(held * nz * (cc * ny + yy), held * nz)]

    def mine(k):
        return db_hbm.at[:, pl.ds(k * step, step), :]

    def remote(src, dst, send, recv, to):
        return pltpu.make_async_remote_copy(
            src_ref=src, dst_ref=dst, send_sem=send, recv_sem=recv, device_id=to, device_id_type=MESH)

    def chain(k, zz, own, upward):
        return remote(mine(k) if own else cell(k, zz, y, core), cell(k, zz, y, core),
                      (up_send if upward else down_send).at[k, zz], z_recv.at[k, zz],
                      {"db": up if upward else down})

    def along_y(k, zz, yy, own):
        return remote(mine(k) if own else cell(k, zz, yy, core), cell(k, zz, yy, core),
                      y_send.at[k, zz], y_recv.at[k, zz], across_y)

    def to_core(k, yy, cc):
        return remote(column(k, yy, cc), column(k, yy, cc), c_send.at[k, yy], c_recv.at[k, yy], sibling)

    def around(k):
        return remote(column(k, other_y, core), column(k, other_y, core), a_send.at[k], a_recv.at[k],
                      {"seq": others_x[0]})

    def weight_rows(xx, cc):
        return w_all.at[pl.ds(pl.multiple_of(xx * w_rows + cc * share, 16), share)]

    def along_x(to, source):
        return remote(w_hbm.at[pl.ds(pl.multiple_of(core * share, 16), share)], weight_rows(source, core),
                      x_send.at[to], x_recv.at[source], {"seq": to})

    def weight_to_core(xx, cc):
        return remote(weight_rows(xx, cc), weight_rows(xx, cc), wc_send.at[xx], wc_recv.at[xx], sibling)

    def through_y(k, do):
        if ny > 1:
            if k in skipper:
                pl.when(x != skipper[k])(do)
            else:
                do()

    def send_own(k):
        pl.when(z < nz - 1)(lambda: chain(k, z, True, True).start())
        pl.when(z > 0)(lambda: chain(k, z, True, False).start())
        through_y(k, lambda: along_y(k, z, y, True).start())

    def pass_z(k):
        @pl.loop(1, nz)
        def _(t):
            @pl.when(z - t >= 0)
            def _():
                chain(k, z - t, False, True).wait_recv()
                pl.when(z < nz - 1)(lambda: chain(k, z - t, False, True).start())
                through_y(k, lambda: along_y(k, z - t, y, False).start())

            @pl.when(z + t < nz)
            def _():
                chain(k, z + t, False, False).wait_recv()
                pl.when(z > 0)(lambda: chain(k, z + t, False, False).start())
                through_y(k, lambda: along_y(k, z + t, y, False).start())
        if nc > 1:
            stay[k].wait()
            to_core(k, y, core).start()

    def pass_y(k):
        def arrive():
            @pl.loop(0, nz)
            def _(zz):
                along_y(k, zz, other_y, False).wait_recv()
            if nc > 1:
                to_core(k, other_y, core).start()
            if k in skipper:
                around(k).start()
        through_y(k, arrive)

    def pass_x(k):
        if k in skipper:
            @pl.when(x == skipper[k])
            def _():
                around(k).wait_recv()
                if nc > 1:
                    to_core(k, other_y, core).start()

    def pass_core(k):
        if nc > 1:
            for yy in range(ny):
                to_core(k, yy, other_core).wait_recv()
        else:
            stay[k].wait()

    ids = remote(ids_ref, ids_in, i_send, i_recv, {"seq": lax.rem(x + 1, nx)})
    stay = [pltpu.make_async_copy(mine(k), cell(k, z, y, core), local.at[k]) for k in range(parts)]
    rest = [
        pltpu.make_async_copy(
            w_hbm, w_all.at[pl.ds(pl.multiple_of(x * w_rows, 16), w_rows)], local.at[parts]),
        pltpu.make_async_copy(q_hbm.at[0], q_all, local.at[parts + 1]),
        pltpu.make_async_copy(ids_ref, ids_own_s, local.at[parts + 2]),
    ]
    ids.start()
    ahead = 3
    for k in range(min(ahead, parts)):
        send_own(k)
        if k == 0:
            for xx in others_x:
                along_x(xx, x).start()
    for copy in stay + rest:
        copy.start()
    ids.wait()
    inward = pltpu.make_async_copy(ids_in, ids_in_s, local.at[parts + 3])
    inward.start()
    inward.wait()
    for copy in rest:
        copy.wait()

    def project(k):
        for j in range(slots):
            if j < KNN:
                block = gathered[k][ids_in_s[0, slots - KNN + j]]
                block = jnp.where(x > 0, block, jnp.zeros_like(block))
            else:
                block = gathered[k][ids_own_s[0, j - KNN]]
            rows[j * step:(j + 1) * step, :] = block
        tile = 512

        @pl.loop(0, cols // tile)
        def _(t):
            at = pl.ds(pl.multiple_of(t * tile, tile), tile)
            got = jnp.dot(rows[...], w_all[:, at], preferred_element_type=jnp.float32)
            kv[:, k * step:(k + 1) * step, at] = got.astype(jnp.bfloat16).reshape(slots, step, tile)

    late = min(4, parts - 1)
    done = 0
    for k in range(parts):
        if k + ahead < parts:
            send_own(k + ahead)
        pass_z(k)
        if k > 0:
            pass_y(k - 1)
        if k == late:
            for xx in others_x:
                along_x(x, xx).wait_recv()
                if nc > 1:
                    weight_to_core(xx, core).start()
            if nc > 1:
                for xx in others_x:
                    weight_to_core(xx, other_core).wait_recv()
        if k >= late:
            for _ in range(1 if k == late else 2):
                if done < k - 1:
                    pass_x(done)
                    pass_core(done)
                    project(done)
                    done += 1
    pass_y(parts - 1)
    for k in range(done, parts):
        pass_x(k)
        pass_core(k)
        project(k)

    @pl.loop(0, stretches)
    def _(c):
        tok = pl.ds(pl.multiple_of(c * length, length), length)
        heads, group = width // HD, 8
        sets = [range(at, min(at + group, heads)) for at in range(0, heads, group)]
        scores, probs = {}, {}
        for turn in range(len(sets) + 2):
            if turn < len(sets):
                for h in sets[turn]:
                    query = q_all[tok, h * HD:(h + 1) * HD]
                    keys = kv[pl.ds(c * KNN, KNN), :, h * HD:(h + 1) * HD].reshape(span, HD)
                    scores[h] = lax.dot_general(
                        query, keys, (((1,), (1,)), ((), ())), preferred_element_type=jnp.float32)
            if 1 <= turn <= len(sets):
                now = sets[turn - 1]
                top = {h: jnp.max(scores[h], axis=-1, keepdims=True) for h in now}
                weights = {h: jnp.exp((scores[h] - top[h]) * HD ** (-0.5)) for h in now}
                total = {h: jnp.sum(weights[h], axis=-1, keepdims=True) for h in now}
                for h in now:
                    probs[h] = (weights[h] * (1.0 / total[h])).astype(jnp.bfloat16)
            if turn >= 2:
                for h in sets[turn - 2]:
                    values = kv[pl.ds(c * KNN, KNN), :, width + h * HD:width + (h + 1) * HD].reshape(span, HD)
                    mixed = jnp.dot(probs[h], values, preferred_element_type=jnp.float32)
                    out_ref[0, tok, h * HD:(h + 1) * HD] = mixed.astype(jnp.bfloat16)
    for k in range(parts):
        @pl.loop(0, nz)
        def _(zz):
            pl.when((z < nz - 1) & (zz <= z))(lambda: chain(k, zz, False, True).wait_send())
            pl.when((z > 0) & (zz >= z))(lambda: chain(k, zz, False, False).wait_send())
            through_y(k, lambda: along_y(k, zz, y, False).wait_send())
        if nc > 1:
            for yy in range(ny):
                to_core(k, yy, core).wait_send()
        if k in skipper:
            pl.when(x != skipper[k])(lambda: around(k).wait_send())
    for xx in others_x:
        along_x(xx, x).wait_send()
        if nc > 1:
            weight_to_core(xx, core).wait_send()


def solution(mesh):
    n_db, nx = mesh.shape["db"], mesh.shape["seq"]
    nc = 2 if mesh.shape["mp"] == 1 and n_db % 2 == 0 else 1
    ny = 2 if mesh.shape["groups"] == 1 and (n_db // nc) % 2 == 0 else 1
    nz = n_db // (nc * ny)
    parts = 8

    def per_device(queries, database, nb_owner, nb_row, kv_weight):
        held, tokens, enc = database.shape
        slots = nb_owner.shape[1]
        w_rows, _, head_cols = kv_weight.shape
        weight = kv_weight.reshape(w_rows, 2 * head_cols)
        zy, core = nb_owner // nc, nb_owner % nc
        place = (core * ny + zy % ny) * nz + zy // ny
        ids = jnp.pad(place * held + nb_row, ((0, 7), (0, 128 - slots)))
        step = tokens // parts
        anywhere = pl.BlockSpec(memory_space=pl.ANY)
        vmem = pl.BlockSpec(memory_space=pltpu.VMEM)
        sem = pltpu.SemaphoreType.DMA
        flops = 2 * slots * tokens * enc * 2 * head_cols
        return pl.pallas_call(
            functools.partial(attend, nz, ny, nc, nx, parts),
            out_shape=jax.ShapeDtypeStruct(queries.shape, jnp.bfloat16),
            in_specs=[anywhere, anywhere, vmem, anywhere],
            out_specs=vmem,
            scratch_shapes=[pltpu.VMEM((n_db * held, step, enc), jnp.bfloat16) for _ in range(parts)] + [
                pltpu.VMEM((nx * w_rows, 2 * head_cols), jnp.bfloat16),
                pltpu.VMEM((slots, tokens, 2 * head_cols), jnp.bfloat16),
                pltpu.VMEM(queries.shape[1:], jnp.bfloat16),
                pltpu.VMEM((slots * step, enc), jnp.bfloat16),
                pltpu.VMEM((8, 128), jnp.int32),
                pltpu.SMEM((8, 128), jnp.int32),
                pltpu.SMEM((8, 128), jnp.int32),
                sem((parts, nz)), sem((parts, nz)), sem((parts, nz)),
                sem((parts, nz)), sem((parts, nz)),
                sem((parts, ny)), sem((parts, ny)),
                sem((parts,)), sem((parts,)),
                sem((nx,)), sem((nx,)),
                sem((nx,)), sem((nx,)),
                sem, sem,
                sem((parts + 4,)),
            ],
            compiler_params=pltpu.CompilerParams(
                collective_id=0, has_side_effects=True, vmem_limit_bytes=60 * 2 ** 20),
            cost_estimate=pl.CostEstimate(flops=flops, bytes_accessed=20 * 2 ** 20, transcendentals=0),
        )(queries, database, ids, weight)

    return jax.shard_map(
        per_device,
        mesh=mesh,
        in_specs=(
            P(("groups", "db"), "seq", "mp"),
            P(("groups", "db"), None, None),
            P(("groups", "db"), "seq"),
            P(("groups", "db"), "seq"),
            P("seq", None, "mp"),
        ),
        out_specs=P(("groups", "db"), "seq", "mp"),
        check_vma=False,
    )
```

```python
import functools

import jax
import jax.numpy as jnp
from jax import lax
from jax.experimental import pallas as pl
from jax.experimental.pallas import tpu as pltpu
from jax.sharding import PartitionSpec as P

HD = 128
KNN = 2
MESH = pl.DeviceIdType.MESH


def attend(nz, ny, nc, nx, parts, *refs):
    q_hbm, db_hbm, ids_ref, w_hbm, out_ref = refs[:5]
    gathered = refs[5:5 + parts]
    (w_all, kv, q_all, rows, ids_in, ids_own_s, ids_in_s, up_send, down_send, z_recv, y_send, y_recv,
     c_send, c_recv, a_send, a_recv, x_send, x_recv, wc_send, wc_recv, i_send, i_recv, local) = refs[5 + parts:]
    d = lax.axis_index("db")
    x = lax.axis_index("seq")
    core = lax.rem(d, nc)
    y = lax.rem(d // nc, ny)
    z = d // (nc * ny)
    held, tokens, enc = db_hbm.shape
    step = tokens // parts
    w_rows = w_hbm.shape[0]
    share = w_rows // nc
    slots = kv.shape[0]
    span = KNN * tokens
    cols = w_all.shape[1]
    width = cols // 2
    stretches = slots // KNN
    length = q_all.shape[0] // stretches
    other_y = lax.rem(y + 1, ny)
    other_core = lax.rem(core + 1, nc)
    skips = {0: (1, 3), 1: (2, 4)} if ny > 1 and nx == 2 and parts > 4 else {}
    skipper = {k: xx for xx, ks in skips.items() for k in ks}

    def index(zz, yy, cc):
        return (zz * ny + yy) * nc + cc

    others_x = [lax.rem(x + r, nx) for r in range(1, nx)]
    up, down = index(z + 1, y, core), index(z - 1, y, core)
    sibling = {"db": index(z, y, other_core)}
    across_y = {"db": index(z, other_y, core)}

    barrier = pltpu.get_barrier_semaphore()
    peers = [{"seq": xx} for xx in others_x]
    if ny > 1:
        peers.append(across_y)
    if nc > 1:
        peers.append(sibling)
    for peer in peers:
        pl.semaphore_signal(barrier, inc=1, device_id=peer, device_id_type=MESH)

    @pl.when(z < nz - 1)
    def _():
        pl.semaphore_signal(barrier, inc=1, device_id={"db": up}, device_id_type=MESH)

    @pl.when(z > 0)
    def _():
        pl.semaphore_signal(barrier, inc=1, device_id={"db": down}, device_id_type=MESH)

    ends = jnp.where(z == 0, 1, 0) + jnp.where(z == nz - 1, 1, 0)
    pl.semaphore_wait(barrier, len(peers) + 2 - ends)

    def cell(k, zz, yy, cc):
        return gathered[k].at[pl.ds(held * ((cc * ny + yy) * nz + zz), held)]

    def column(k, yy, cc):
        return gathered[k].at[pl.ds(held * nz * (cc * ny + yy), held * nz)]

    def mine(k):
        return db_hbm.at[:, pl.ds(k * step, step), :]

    def remote(src, dst, send, recv, to):
        return pltpu.make_async_remote_copy(
            src_ref=src, dst_ref=dst, send_sem=send, recv_sem=recv, device_id=to, device_id_type=MESH)

    def chain(k, zz, own, upward):
        return remote(mine(k) if own else cell(k, zz, y, core), cell(k, zz, y, core),
                      (up_send if upward else down_send).at[k, zz], z_recv.at[k, zz],
                      {"db": up if upward else down})

    def along_y(k, zz, yy, own):
        return remote(mine(k) if own else cell(k, zz, yy, core), cell(k, zz, yy, core),
                      y_send.at[k, zz], y_recv.at[k, zz], across_y)

    def to_core(k, yy, cc):
        return remote(column(k, yy, cc), column(k, yy, cc), c_send.at[k, yy], c_recv.at[k, yy], sibling)

    def around(k):
        return remote(column(k, other_y, core), column(k, other_y, core), a_send.at[k], a_recv.at[k],
                      {"seq": others_x[0]})

    def weight_rows(xx, cc):
        return w_all.at[pl.ds(pl.multiple_of(xx * w_rows + cc * share, 16), share)]

    def along_x(to, source):
        return remote(w_hbm.at[pl.ds(pl.multiple_of(core * share, 16), share)], weight_rows(source, core),
                      x_send.at[to], x_recv.at[source], {"seq": to})

    def weight_to_core(xx, cc):
        return remote(weight_rows(xx, cc), weight_rows(xx, cc), wc_send.at[xx], wc_recv.at[xx], sibling)

    def through_y(k, do):
        if ny > 1:
            if k in skipper:
                pl.when(x != skipper[k])(do)
            else:
                do()

    def send_own(k):
        pl.when(z < nz - 1)(lambda: chain(k, z, True, True).start())
        pl.when(z > 0)(lambda: chain(k, z, True, False).start())
        through_y(k, lambda: along_y(k, z, y, True).start())

    def pass_z(k, beside):
        def hop(t):
            @pl.when(z - t >= 0)
            def _():
                chain(k, z - t, False, True).wait_recv()
                pl.when(z < nz - 1)(lambda: chain(k, z - t, False, True).start())
                through_y(k, lambda: along_y(k, z - t, y, False).start())

            @pl.when(z + t < nz)
            def _():
                chain(k, z + t, False, False).wait_recv()
                pl.when(z > 0)(lambda: chain(k, z + t, False, False).start())
                through_y(k, lambda: along_y(k, z + t, y, False).start())

        hops = nz - 1
        if beside and hops < 8:
            for t in range(1, nz):
                hop(t)
                for work in beside[(t - 1) * len(beside) // hops:t * len(beside) // hops]:
                    work()
        else:
            pl.loop(1, nz)(hop)
            for work in beside:
                work()
        if nc > 1:
            stay[k].wait()
            to_core(k, y, core).start()

    def pass_y(k):
        def arrive():
            @pl.loop(0, nz)
            def _(zz):
                along_y(k, zz, other_y, False).wait_recv()
            if nc > 1:
                to_core(k, other_y, core).start()
            if k in skipper:
                around(k).start()
        through_y(k, arrive)

    def pass_x(k):
        if k in skipper:
            @pl.when(x == skipper[k])
            def _():
                around(k).wait_recv()
                if nc > 1:
                    to_core(k, other_y, core).start()

    def pass_core(k):
        if nc > 1:
            for yy in range(ny):
                to_core(k, yy, other_core).wait_recv()
        else:
            stay[k].wait()

    ids = remote(ids_ref, ids_in, i_send, i_recv, {"seq": lax.rem(x + 1, nx)})
    stay = [pltpu.make_async_copy(mine(k), cell(k, z, y, core), local.at[k]) for k in range(parts)]
    rest = [
        pltpu.make_async_copy(
            w_hbm, w_all.at[pl.ds(pl.multiple_of(x * w_rows, 16), w_rows)], local.at[parts]),
        pltpu.make_async_copy(q_hbm.at[0], q_all, local.at[parts + 1]),
        pltpu.make_async_copy(ids_ref, ids_own_s, local.at[parts + 2]),
    ]
    ids.start()
    ahead = 3
    for k in range(min(ahead, parts)):
        send_own(k)
        if k == 0:
            for xx in others_x:
                along_x(xx, x).start()
    for copy in stay + rest:
        copy.start()
    ids.wait()
    inward = pltpu.make_async_copy(ids_in, ids_in_s, local.at[parts + 3])
    inward.start()
    inward.wait()
    for copy in rest:
        copy.wait()

    def pick(k):
        for j in range(slots):
            if j < KNN:
                block = gathered[k][ids_in_s[0, slots - KNN + j]]
                block = jnp.where(x > 0, block, jnp.zeros_like(block))
            else:
                block = gathered[k][ids_own_s[0, j - KNN]]
            rows[j * step:(j + 1) * step, :] = block

    tile = 512
    tiles = cols // tile

    def project(k, first, last):
        @pl.loop(first, last)
        def _(t):
            at = pl.ds(pl.multiple_of(t * tile, tile), tile)
            got = jnp.dot(rows[...], w_all[:, at], preferred_element_type=jnp.float32)
            kv[:, k * step:(k + 1) * step, at] = got.astype(jnp.bfloat16).reshape(slots, step, tile)

    def steps_of(k):
        def begin():
            pass_x(k)
            pass_core(k)
            pick(k)
        return [begin] + [functools.partial(project, k, t, t + 2) for t in range(0, tiles, 2)]

    late = min(4, parts - 1)
    done = 0
    for k in range(parts):
        if k + ahead < parts:
            send_own(k + ahead)
        beside = []
        if k > late:
            for _ in range(2):
                if done < k - 1:
                    beside += steps_of(done)
                    done += 1
        pass_z(k, beside)
        if k > 0:
            pass_y(k - 1)
        if k == late:
            for xx in others_x:
                along_x(x, xx).wait_recv()
                if nc > 1:
                    weight_to_core(xx, core).start()
            if nc > 1:
                for xx in others_x:
                    weight_to_core(xx, other_core).wait_recv()
    for k in range(done, parts):
        if k == parts - 1:
            pass_y(k)
        for work in steps_of(k):
            work()

    @pl.loop(0, stretches)
    def _(c):
        tok = pl.ds(pl.multiple_of(c * length, length), length)
        heads, group = width // HD, 8
        sets = [range(at, min(at + group, heads)) for at in range(0, heads, group)]
        scores, probs = {}, {}
        for turn in range(len(sets) + 2):
            if turn < len(sets):
                for h in sets[turn]:
                    query = q_all[tok, h * HD:(h + 1) * HD]
                    keys = kv[pl.ds(c * KNN, KNN), :, h * HD:(h + 1) * HD].reshape(span, HD)
                    scores[h] = lax.dot_general(
                        query, keys, (((1,), (1,)), ((), ())), preferred_element_type=jnp.float32)
            if 1 <= turn <= len(sets):
                now = sets[turn - 1]
                top = {h: jnp.max(scores[h], axis=-1, keepdims=True) for h in now}
                weights = {h: jnp.exp((scores[h] - top[h]) * HD ** (-0.5)) for h in now}
                total = {h: jnp.sum(weights[h], axis=-1, keepdims=True) for h in now}
                for h in now:
                    probs[h] = (weights[h] * (1.0 / total[h])).astype(jnp.bfloat16)
            if turn >= 2:
                for h in sets[turn - 2]:
                    values = kv[pl.ds(c * KNN, KNN), :, width + h * HD:width + (h + 1) * HD].reshape(span, HD)
                    mixed = jnp.dot(probs[h], values, preferred_element_type=jnp.float32)
                    out_ref[0, tok, h * HD:(h + 1) * HD] = mixed.astype(jnp.bfloat16)
    for k in range(parts):
        @pl.loop(0, nz)
        def _(zz):
            pl.when((z < nz - 1) & (zz <= z))(lambda: chain(k, zz, False, True).wait_send())
            pl.when((z > 0) & (zz >= z))(lambda: chain(k, zz, False, False).wait_send())
            through_y(k, lambda: along_y(k, zz, y, False).wait_send())
        if nc > 1:
            for yy in range(ny):
                to_core(k, yy, core).wait_send()
        if k in skipper:
            pl.when(x != skipper[k])(lambda: around(k).wait_send())
    for xx in others_x:
        along_x(xx, x).wait_send()
        if nc > 1:
            weight_to_core(xx, core).wait_send()


def solution(mesh):
    n_db, nx = mesh.shape["db"], mesh.shape["seq"]
    nc = 2 if mesh.shape["mp"] == 1 and n_db % 2 == 0 else 1
    ny = 2 if mesh.shape["groups"] == 1 and (n_db // nc) % 2 == 0 else 1
    nz = n_db // (nc * ny)
    parts = 8

    def per_device(queries, database, nb_owner, nb_row, kv_weight):
        held, tokens, enc = database.shape
        slots = nb_owner.shape[1]
        w_rows, _, head_cols = kv_weight.shape
        weight = kv_weight.reshape(w_rows, 2 * head_cols)
        zy, core = nb_owner // nc, nb_owner % nc
        place = (core * ny + zy % ny) * nz + zy // ny
        ids = jnp.pad(place * held + nb_row, ((0, 7), (0, 128 - slots)))
        step = tokens // parts
        anywhere = pl.BlockSpec(memory_space=pl.ANY)
        vmem = pl.BlockSpec(memory_space=pltpu.VMEM)
        sem = pltpu.SemaphoreType.DMA
        flops = 2 * slots * tokens * enc * 2 * head_cols
        return pl.pallas_call(
            functools.partial(attend, nz, ny, nc, nx, parts),
            out_shape=jax.ShapeDtypeStruct(queries.shape, jnp.bfloat16),
            in_specs=[anywhere, anywhere, vmem, anywhere],
            out_specs=vmem,
            scratch_shapes=[pltpu.VMEM((n_db * held, step, enc), jnp.bfloat16) for _ in range(parts)] + [
                pltpu.VMEM((nx * w_rows, 2 * head_cols), jnp.bfloat16),
                pltpu.VMEM((slots, tokens, 2 * head_cols), jnp.bfloat16),
                pltpu.VMEM(queries.shape[1:], jnp.bfloat16),
                pltpu.VMEM((slots * step, enc), jnp.bfloat16),
                pltpu.VMEM((8, 128), jnp.int32),
                pltpu.SMEM((8, 128), jnp.int32),
                pltpu.SMEM((8, 128), jnp.int32),
                sem((parts, nz)), sem((parts, nz)), sem((parts, nz)),
                sem((parts, nz)), sem((parts, nz)),
                sem((parts, ny)), sem((parts, ny)),
                sem((parts,)), sem((parts,)),
                sem((nx,)), sem((nx,)),
                sem((nx,)), sem((nx,)),
                sem, sem,
                sem((parts + 4,)),
            ],
            compiler_params=pltpu.CompilerParams(
                collective_id=0, has_side_effects=True, vmem_limit_bytes=60 * 2 ** 20),
            cost_estimate=pl.CostEstimate(flops=flops, bytes_accessed=20 * 2 ** 20, transcendentals=0),
        )(queries, database, ids, weight)

    return jax.shard_map(
        per_device,
        mesh=mesh,
        in_specs=(
            P(("groups", "db"), "seq", "mp"),
            P(("groups", "db"), None, None),
            P(("groups", "db"), "seq"),
            P(("groups", "db"), "seq"),
            P("seq", None, "mp"),
        ),
        out_specs=P(("groups", "db"), "seq", "mp"),
        check_vma=False,
    )
```

```python
import functools

import jax
import jax.numpy as jnp
from jax import lax
from jax.experimental import pallas as pl
from jax.experimental.pallas import tpu as pltpu
from jax.sharding import PartitionSpec as P

HD = 128
KNN = 2
MESH = pl.DeviceIdType.MESH


def attend(nz, ny, nc, nx, parts, *refs):
    q_hbm, db_hbm, ids_ref, w_hbm, out_ref = refs[:5]
    gathered = refs[5:5 + parts]
    (w_all, kv, q_all, rows, ids_in, ids_own_s, ids_in_s, up_send, down_send, z_recv, y_send, y_recv,
     c_send, c_recv, a_send, a_recv, x_send, x_recv, wc_send, wc_recv, i_send, i_recv, local) = refs[5 + parts:]
    d = lax.axis_index("db")
    x = lax.axis_index("seq")
    core = lax.rem(d, nc)
    y = lax.rem(d // nc, ny)
    z = d // (nc * ny)
    held, tokens, enc = db_hbm.shape
    step = tokens // parts
    w_rows = w_hbm.shape[0]
    share = w_rows // nc
    slots = kv.shape[0]
    span = KNN * tokens
    cols = w_all.shape[1]
    width = cols // 2
    stretches = slots // KNN
    length = q_all.shape[0] // stretches
    other_y = lax.rem(y + 1, ny)
    other_core = lax.rem(core + 1, nc)
    skips = {0: (1, 3), 1: (2, 4)} if ny > 1 and nx == 2 and parts > 4 else {}
    skipper = {k: xx for xx, ks in skips.items() for k in ks}

    def index(zz, yy, cc):
        return (zz * ny + yy) * nc + cc

    others_x = [lax.rem(x + r, nx) for r in range(1, nx)]
    up, down = index(z + 1, y, core), index(z - 1, y, core)
    sibling = {"db": index(z, y, other_core)}
    across_y = {"db": index(z, other_y, core)}

    barrier = pltpu.get_barrier_semaphore()
    peers = [{"seq": xx} for xx in others_x]
    if ny > 1:
        peers.append(across_y)
    if nc > 1:
        peers.append(sibling)
    for peer in peers:
        pl.semaphore_signal(barrier, inc=1, device_id=peer, device_id_type=MESH)

    @pl.when(z < nz - 1)
    def _():
        pl.semaphore_signal(barrier, inc=1, device_id={"db": up}, device_id_type=MESH)

    @pl.when(z > 0)
    def _():
        pl.semaphore_signal(barrier, inc=1, device_id={"db": down}, device_id_type=MESH)

    ends = jnp.where(z == 0, 1, 0) + jnp.where(z == nz - 1, 1, 0)
    pl.semaphore_wait(barrier, len(peers) + 2 - ends)

    def cell(k, zz, yy, cc):
        return gathered[k].at[pl.ds(held * ((cc * ny + yy) * nz + zz), held)]

    def column(k, yy, cc):
        return gathered[k].at[pl.ds(held * nz * (cc * ny + yy), held * nz)]

    def mine(k):
        return db_hbm.at[:, pl.ds(k * step, step), :]

    def remote(src, dst, send, recv, to):
        return pltpu.make_async_remote_copy(
            src_ref=src, dst_ref=dst, send_sem=send, recv_sem=recv, device_id=to, device_id_type=MESH)

    def chain(k, zz, own, upward):
        return remote(mine(k) if own else cell(k, zz, y, core), cell(k, zz, y, core),
                      (up_send if upward else down_send).at[k, zz], z_recv.at[k, zz],
                      {"db": up if upward else down})

    def along_y(k, zz, yy, own):
        return remote(mine(k) if own else cell(k, zz, yy, core), cell(k, zz, yy, core),
                      y_send.at[k, zz], y_recv.at[k, zz], across_y)

    def to_core(k, yy, cc):
        return remote(column(k, yy, cc), column(k, yy, cc), c_send.at[k, yy], c_recv.at[k, yy], sibling)

    def around(k):
        return remote(column(k, other_y, core), column(k, other_y, core), a_send.at[k], a_recv.at[k],
                      {"seq": others_x[0]})

    def weight_rows(xx, cc):
        return w_all.at[pl.ds(pl.multiple_of(xx * w_rows + cc * share, 16), share)]

    def along_x(to, source):
        return remote(w_hbm.at[pl.ds(pl.multiple_of(core * share, 16), share)], weight_rows(source, core),
                      x_send.at[to], x_recv.at[source], {"seq": to})

    def weight_to_core(xx, cc):
        return remote(weight_rows(xx, cc), weight_rows(xx, cc), wc_send.at[xx], wc_recv.at[xx], sibling)

    def through_y(k, do):
        if ny > 1:
            if k in skipper:
                pl.when(x != skipper[k])(do)
            else:
                do()

    def send_own(k):
        pl.when(z < nz - 1)(lambda: chain(k, z, True, True).start())
        pl.when(z > 0)(lambda: chain(k, z, True, False).start())
        through_y(k, lambda: along_y(k, z, y, True).start())

    def pass_z(k, beside):
        def hop(t):
            @pl.when(z - t >= 0)
            def _():
                chain(k, z - t, False, True).wait_recv()
                pl.when(z < nz - 1)(lambda: chain(k, z - t, False, True).start())
                through_y(k, lambda: along_y(k, z - t, y, False).start())

            @pl.when(z + t < nz)
            def _():
                chain(k, z + t, False, False).wait_recv()
                pl.when(z > 0)(lambda: chain(k, z + t, False, False).start())
                through_y(k, lambda: along_y(k, z + t, y, False).start())

        hops = nz - 1
        if beside and hops < 8:
            for t in range(1, nz):
                hop(t)
                for work in beside[(t - 1) * len(beside) // hops:t * len(beside) // hops]:
                    work()
        else:
            pl.loop(1, nz)(hop)
            for work in beside:
                work()
        if nc > 1:
            stay[k].wait()
            to_core(k, y, core).start()

    def pass_y(k):
        def arrive():
            @pl.loop(0, nz)
            def _(zz):
                along_y(k, zz, other_y, False).wait_recv()
            if nc > 1:
                to_core(k, other_y, core).start()
            if k in skipper:
                around(k).start()
        through_y(k, arrive)

    def pass_x(k):
        if k in skipper:
            @pl.when(x == skipper[k])
            def _():
                around(k).wait_recv()
                if nc > 1:
                    to_core(k, other_y, core).start()

    def pass_core(k):
        if nc > 1:
            for yy in range(ny):
                to_core(k, yy, other_core).wait_recv()
        else:
            stay[k].wait()

    ids = remote(ids_ref, ids_in, i_send, i_recv, {"seq": lax.rem(x + 1, nx)})
    stay = [pltpu.make_async_copy(mine(k), cell(k, z, y, core), local.at[k]) for k in range(parts)]
    rest = [
        pltpu.make_async_copy(
            w_hbm, w_all.at[pl.ds(pl.multiple_of(x * w_rows, 16), w_rows)], local.at[parts]),
        pltpu.make_async_copy(q_hbm.at[0], q_all, local.at[parts + 1]),
        pltpu.make_async_copy(ids_ref, ids_own_s, local.at[parts + 2]),
    ]
    ids.start()
    ahead = 3
    for k in range(min(ahead, parts)):
        send_own(k)
        if k == 0:
            for xx in others_x:
                along_x(xx, x).start()
    for copy in stay + rest:
        copy.start()
    ids.wait()
    inward = pltpu.make_async_copy(ids_in, ids_in_s, local.at[parts + 3])
    inward.start()
    inward.wait()
    for copy in rest:
        copy.wait()

    def pick(k):
        for j in range(slots):
            if j < KNN:
                block = gathered[k][ids_in_s[0, slots - KNN + j]]
                block = jnp.where(x > 0, block, jnp.zeros_like(block))
            else:
                block = gathered[k][ids_own_s[0, j - KNN]]
            rows[j * step:(j + 1) * step, :] = block

    tile = 1024
    tiles = cols // tile

    def project(k, first, last):
        @pl.loop(first, last)
        def _(t):
            at = pl.ds(pl.multiple_of(t * tile, tile), tile)
            got = jnp.dot(rows[...], w_all[:, at], preferred_element_type=jnp.float32)
            kv[:, k * step:(k + 1) * step, at] = got.astype(jnp.bfloat16).reshape(slots, step, tile)

    def steps_of(k):
        def begin():
            pass_x(k)
            pass_core(k)
            pick(k)
        return [begin] + [functools.partial(project, k, t, t + 1) for t in range(0, tiles, 1)]

    late = min(4, parts - 1)
    done = 0
    for k in range(parts):
        if k + ahead < parts:
            send_own(k + ahead)
        beside = []
        if k > late:
            for _ in range(2):
                if done < k - 1:
                    beside += steps_of(done)
                    done += 1
        pass_z(k, beside)
        if k > 0:
            pass_y(k - 1)
        if k == late:
            for xx in others_x:
                along_x(x, xx).wait_recv()
                if nc > 1:
                    weight_to_core(xx, core).start()
            if nc > 1:
                for xx in others_x:
                    weight_to_core(xx, other_core).wait_recv()
    for k in range(done, parts):
        if k == parts - 1:
            pass_y(k)
        for work in steps_of(k):
            work()

    @pl.loop(0, stretches)
    def _(c):
        tok = pl.ds(pl.multiple_of(c * length, length), length)
        heads, group = width // HD, 8
        sets = [range(at, min(at + group, heads)) for at in range(0, heads, group)]
        scores, probs = {}, {}
        for turn in range(len(sets) + 2):
            if turn < len(sets):
                for h in sets[turn]:
                    query = q_all[tok, h * HD:(h + 1) * HD]
                    keys = kv[pl.ds(c * KNN, KNN), :, h * HD:(h + 1) * HD].reshape(span, HD)
                    scores[h] = lax.dot_general(
                        query, keys, (((1,), (1,)), ((), ())), preferred_element_type=jnp.float32)
            if 1 <= turn <= len(sets):
                now = sets[turn - 1]
                top = {h: jnp.max(scores[h], axis=-1, keepdims=True) for h in now}
                weights = {h: jnp.exp((scores[h] - top[h]) * HD ** (-0.5)) for h in now}
                total = {h: jnp.sum(weights[h], axis=-1, keepdims=True) for h in now}
                for h in now:
                    probs[h] = (weights[h] * (1.0 / total[h])).astype(jnp.bfloat16)
            if turn >= 2:
                for h in sets[turn - 2]:
                    values = kv[pl.ds(c * KNN, KNN), :, width + h * HD:width + (h + 1) * HD].reshape(span, HD)
                    mixed = jnp.dot(probs[h], values, preferred_element_type=jnp.float32)
                    out_ref[0, tok, h * HD:(h + 1) * HD] = mixed.astype(jnp.bfloat16)
    for k in range(parts):
        @pl.loop(0, nz)
        def _(zz):
            pl.when((z < nz - 1) & (zz <= z))(lambda: chain(k, zz, False, True).wait_send())
            pl.when((z > 0) & (zz >= z))(lambda: chain(k, zz, False, False).wait_send())
            through_y(k, lambda: along_y(k, zz, y, False).wait_send())
        if nc > 1:
            for yy in range(ny):
                to_core(k, yy, core).wait_send()
        if k in skipper:
            pl.when(x != skipper[k])(lambda: around(k).wait_send())
    for xx in others_x:
        along_x(xx, x).wait_send()
        if nc > 1:
            weight_to_core(xx, core).wait_send()


def solution(mesh):
    n_db, nx = mesh.shape["db"], mesh.shape["seq"]
    nc = 2 if mesh.shape["mp"] == 1 and n_db % 2 == 0 else 1
    ny = 2 if mesh.shape["groups"] == 1 and (n_db // nc) % 2 == 0 else 1
    nz = n_db // (nc * ny)
    parts = 8

    def per_device(queries, database, nb_owner, nb_row, kv_weight):
        held, tokens, enc = database.shape
        slots = nb_owner.shape[1]
        w_rows, _, head_cols = kv_weight.shape
        weight = kv_weight.reshape(w_rows, 2 * head_cols)
        zy, core = nb_owner // nc, nb_owner % nc
        place = (core * ny + zy % ny) * nz + zy // ny
        ids = jnp.pad(place * held + nb_row, ((0, 7), (0, 128 - slots)))
        step = tokens // parts
        anywhere = pl.BlockSpec(memory_space=pl.ANY)
        vmem = pl.BlockSpec(memory_space=pltpu.VMEM)
        sem = pltpu.SemaphoreType.DMA
        flops = 2 * slots * tokens * enc * 2 * head_cols
        return pl.pallas_call(
            functools.partial(attend, nz, ny, nc, nx, parts),
            out_shape=jax.ShapeDtypeStruct(queries.shape, jnp.bfloat16),
            in_specs=[anywhere, anywhere, vmem, anywhere],
            out_specs=vmem,
            scratch_shapes=[pltpu.VMEM((n_db * held, step, enc), jnp.bfloat16) for _ in range(parts)] + [
                pltpu.VMEM((nx * w_rows, 2 * head_cols), jnp.bfloat16),
                pltpu.VMEM((slots, tokens, 2 * head_cols), jnp.bfloat16),
                pltpu.VMEM(queries.shape[1:], jnp.bfloat16),
                pltpu.VMEM((slots * step, enc), jnp.bfloat16),
                pltpu.VMEM((8, 128), jnp.int32),
                pltpu.SMEM((8, 128), jnp.int32),
                pltpu.SMEM((8, 128), jnp.int32),
                sem((parts, nz)), sem((parts, nz)), sem((parts, nz)),
                sem((parts, nz)), sem((parts, nz)),
                sem((parts, ny)), sem((parts, ny)),
                sem((parts,)), sem((parts,)),
                sem((nx,)), sem((nx,)),
                sem((nx,)), sem((nx,)),
                sem, sem,
                sem((parts + 4,)),
            ],
            compiler_params=pltpu.CompilerParams(
                collective_id=0, has_side_effects=True, vmem_limit_bytes=60 * 2 ** 20),
            cost_estimate=pl.CostEstimate(flops=flops, bytes_accessed=20 * 2 ** 20, transcendentals=0),
        )(queries, database, ids, weight)

    return jax.shard_map(
        per_device,
        mesh=mesh,
        in_specs=(
            P(("groups", "db"), "seq", "mp"),
            P(("groups", "db"), None, None),
            P(("groups", "db"), "seq"),
            P(("groups", "db"), "seq"),
            P("seq", None, "mp"),
        ),
        out_specs=P(("groups", "db"), "seq", "mp"),
        check_vma=False,
    )
```
